32 devices in a mesh: rows: 4 (over y, x), cand: 8 (over z, core).
Axes of the slice: x: 2, y: 2, z: 4, core: 2. Of those that a mesh axis runs over, the one named last changes fastest.
Arguments:
- whitened: float32 [256, 2048], P('cand', 'rows'), may hold values from -6 to 6
- factor_rows: float32 [2048, 2048], P('rows'), as said below
- diag_inv: float32 [2048, 512], P('rows'), as said below
- observed: float32 [22, 2048], P(None, 'rows'), may hold values from 0 to 1
- inv_length: float32 [22], replicated, may hold values from 0.4 to 2
- grid_coords: int32 [22, 32768], P(None, 'cand'), may hold values from 0 to 20
- frequencies: float32 [22, 8192], P(None, 'rows'), may hold values from -8 to 8
- phases: float32 [8192], P('rows'), may hold values from -3.140625 to 3.140625
- prior_coef: bfloat16 [256, 8192], P('cand', 'rows'), may hold values from -6 to 6
Outputs:
- samples_at: float32 [32768, 256], P('cand', 'rows')
The draws below stay inside these ranges and needn't reach their ends.
Inputs may be any that keep to these rules, and one draw needn't show every extreme that they name: `factor_rows`: entries in and above the diagonal blocks of 512 x 512 are zero. `diag_inv`: each block of 512 rows is lower triangular with a positive diagonal.
All inputs are finite; a program needn't handle non-finite values.
Results may differ from the reference program's by a relative error of at most 0.004.
Values may be sent and summed in bfloat16 or wider, within the bound.
A program may use at most 320 MiB of HBM per device.

```python
import math
import jax
import jax.numpy as jnp
from jax import lax

DIM = 22
FEAT = 8192
SAMPLES = 256
BLOCK = 512
GRID = 21
CAND_DEV = 4096
OBS = 2048
CANDS = 32768


def draw_factor_rows(key, part):
    row_block = jnp.arange(OBS)[:, None] // BLOCK
    col_block = jnp.arange(OBS)[None, :] // BLOCK
    below = (row_block > col_block).astype(jnp.float32)
    values = jax.random.uniform(key, (OBS, OBS), jnp.float32, -0.8, 0.8)
    return values * below / jnp.sqrt(jnp.float32(OBS))


def draw_diag_inv(key, part):
    first_key, second_key = jax.random.split(key)
    row_local = jnp.arange(OBS)[:, None] % BLOCK
    column = jnp.arange(BLOCK)[None, :]
    lower = (column < row_local).astype(jnp.float32)
    on_diagonal = column == row_local
    spread = jax.random.uniform(first_key, (OBS, BLOCK), jnp.float32, -0.8, 0.8) / jnp.sqrt(jnp.float32(BLOCK))
    leading = jax.random.uniform(second_key, (OBS, BLOCK), jnp.float32, 0.6, 1.2)
    return spread * lower + jnp.where(on_diagonal, leading, 0.0)


def set_ends(values, rng, smallest, high):
    spot = [jax.random.randint(jax.random.fold_in(rng, axis), (), 0, length) for axis, length in enumerate(values.shape)]
    longest = values.shape.index(max(values.shape))
    neighbour = spot[:longest] + [(spot[longest] + 1) % values.shape[longest]] + spot[longest + 1:]
    return values.at[tuple(spot)].set(smallest).at[tuple(neighbour)].set(high)


def shard_levels(stream_key, extent, cuts, low, high):
    factor_of = 1.0
    for position, blocks in cuts:
        heights = jax.random.uniform(jax.random.fold_in(jax.random.fold_in(stream_key, 6), position), (blocks,), jnp.float32, low / len(cuts), high / len(cuts))
        factor_of = factor_of * jnp.repeat(jnp.exp(heights), extent[position] // blocks).reshape((-1,) + (1,) * (len(extent) - 1 - position))
    return factor_of


def centred(own_key, shape, deviation, bound, cuts=(), held_as=jnp.bfloat16):
    array = jax.random.normal(own_key, shape, jnp.float32) * deviation
    if len(cuts) > 0:
        array = shard_levels(own_key, shape, cuts, -0.22, 0.18) * array
    return jnp.clip(array, min=-bound, max=bound).astype(held_as)


def setup_inputs(seed: int = 0) -> dict:
    key_of = jax.random.split(jax.random.key(seed), 10)
    return {
        "whitened": centred(key_of[0], (SAMPLES, OBS), 1.0, 6.0, ((0, 8), (1, 4)), jnp.float32),
        "factor_rows": draw_factor_rows(jax.random.fold_in(key_of[9], 71), 0),
        "diag_inv": draw_diag_inv(jax.random.fold_in(key_of[9], 71), 0),
        "observed": jnp.clip(1.0 * jax.random.uniform(key_of[3], (DIM, OBS), jnp.float32) ** shard_levels(key_of[3], (DIM, OBS), ((1, 4),), -0.2, 0.2), 0.0, 1.0),
        "inv_length": jnp.clip(jnp.exp(jax.random.uniform(key_of[4], (DIM,), jnp.float32, math.log(0.4), math.log(2.0))), 0.4, 2.0),
        "grid_coords": set_ends(jax.random.randint(key_of[5], (DIM, CANDS), 0, GRID), jax.random.fold_in(key_of[5], 1), 0, GRID - 1).astype(jnp.int32),
        "frequencies": centred(key_of[6], (DIM, FEAT), 2.0, 8.0, ((1, 4),), jnp.float32),
        "phases": jnp.clip(jax.random.uniform(key_of[7], (FEAT,), jnp.float32, -3.140625, 3.140625), -3.140625, 3.140625),
        "prior_coef": centred(key_of[8], (SAMPLES, FEAT), 1.0, 6.0, ((0, 8), (1, 4))),
    }


def back_solve(whitened, factor_rows, diag_inv):
    carried = jnp.zeros_like(whitened)
    pieces = []
    for block_id in reversed(range(OBS // BLOCK)):
        offset = block_id * BLOCK
        remaining = whitened[:, offset:offset + BLOCK] - carried[:, offset:offset + BLOCK]
        solved = jnp.dot(remaining, diag_inv[offset:offset + BLOCK], precision=lax.Precision.HIGHEST, preferred_element_type=jnp.float32)
        carried = carried + jnp.dot(solved, factor_rows[offset:offset + BLOCK], precision=lax.Precision.HIGHEST, preferred_element_type=jnp.float32)
        pieces.append(solved)
    return jnp.concatenate(pieces[::-1], axis=1)

def evaluate_block(coords_block, weights_wire, observed, inv_length, frequencies, phases, prior_coef):
    mixture = coords_block.astype(jnp.float32) / (GRID - 1)
    angles = jnp.dot(mixture.T, frequencies, precision=lax.Precision.HIGHEST, preferred_element_type=jnp.float32) + phases[None, :]
    features_map = (jnp.sqrt(2.0 / FEAT) * jnp.cos(angles)).astype(jnp.bfloat16)
    prior_part = jnp.dot(features_map, prior_coef.T, preferred_element_type=jnp.float32)
    squared = jnp.zeros((mixture.shape[1], observed.shape[1]), jnp.float32)
    for column in range(DIM):
        gap = (mixture[column][:, None] - observed[column][None, :]) * inv_length[column]
        squared = squared + gap * gap
    kernel_tile = jnp.exp(-0.5 * squared).astype(jnp.bfloat16)
    return prior_part + jnp.dot(kernel_tile, weights_wire.T, preferred_element_type=jnp.float32)

def reference(whitened, factor_rows, diag_inv, observed, inv_length, grid_coords, frequencies, phases, prior_coef):
    weights = back_solve(whitened, factor_rows, diag_inv)
    weights_wire = weights.astype(jnp.bfloat16)
    blocked = jnp.transpose(grid_coords.reshape(DIM, CANDS // CAND_DEV, CAND_DEV), (1, 0, 2))

    def one_block(coords_block):
        return evaluate_block(coords_block, weights_wire, observed, inv_length, frequencies, phases, prior_coef)
    values = lax.map(one_block, blocked)
    return values.reshape(CANDS, SAMPLES)
```

```python
import functools

import jax
import jax.numpy as jnp
import numpy as np
from jax import lax
from jax.experimental import pallas as pl
from jax.experimental.pallas import tpu as pltpu
from jax.sharding import PartitionSpec as P

GRID = 21
CHUNK = 512
FB = 256
DEPTH = 128
HIGH = lax.Precision.HIGHEST
F32 = jnp.float32
BF16 = jnp.bfloat16


def sine_coefficients(terms):
    v = 0.125 * (1 - np.cos(np.pi * (np.arange(400) + 0.5) / 400)) + 1e-9
    rows = np.stack([v ** (2 * i + 1) for i in range(terms)], 1)
    goal = np.sin(2 * np.pi * v)
    return np.linalg.lstsq(rows / goal[:, None], np.ones_like(goal), rcond=None)[0]


def kernel(
    peers_r,
    peers_c,
    scale,
    g_ref,
    ft_ref,
    ot_ref,
    coef_ref,
    x_ref,
    fac_ref,
    dinv_ref,
    out_ref,
    feat,
    coefw,
    cbuf,
    wown,
    wbuf,
    wide,
    csend,
    crecv,
    acc,
    own,
    sbuf,
    rbuf,
    gs,
    gr,
    ws,
    wr,
    cs,
    cr,
    ss,
    sr,
):
    me = lax.axis_index("rows")
    c = lax.axis_index("cand")
    groups = peers_c // 2
    q = c // 2
    core = c % 2
    sibling = q * 2 + (1 - core)
    samples = coef_ref.shape[0]
    nf = ft_ref.shape[0] // FB
    no = ot_ref.shape[0] // FB
    slots = feat.shape[0]
    chunks = out_ref.shape[1] // CHUNK
    part = out_ref.shape[0]
    width = x_ref.shape[1]
    poly = [float(a) * scale for a in sine_coefficients(4)]

    barrier = pltpu.get_barrier_semaphore()
    for d in range(1, peers_r):
        pl.semaphore_signal(
            barrier, inc=1, device_id={"rows": (me + d) % peers_r}, device_id_type=pl.DeviceIdType.MESH
        )
    for d in range(1, groups):
        pl.semaphore_signal(
            barrier,
            inc=1,
            device_id={"cand": ((q + d) % groups) * 2 + core},
            device_id_type=pl.DeviceIdType.MESH,
        )
    pl.semaphore_signal(barrier, inc=1, device_id={"cand": sibling}, device_id_type=pl.DeviceIdType.MESH)
    pl.semaphore_wait(barrier, peers_r - 1 + groups)

    def hop(src, dst, send, recv, cand):
        return pltpu.make_async_remote_copy(
            src_ref=src,
            dst_ref=dst,
            send_sem=send,
            recv_sem=recv,
            device_id={"cand": cand},
            device_id_type=pl.DeviceIdType.MESH,
        )

    def gather_send(mine, buf, send, recv):
        for d in range(1, groups):
            hop(mine, buf.at[c], send.at[d], recv.at[c], ((q + d) % groups) * 2 + core).start()
        hop(mine, buf.at[c], send.at[groups], recv.at[c], sibling).start()
        buf[c] = mine[...]

    def gather_forward(mine, buf, send, recv):
        for d in range(1, groups):
            other = ((q + groups - d) % groups) * 2 + core
            hop(mine, buf.at[other], send.at[d], recv.at[other], sibling).wait_recv()
            hop(buf.at[other], buf.at[other], send.at[groups + d], recv.at[other], sibling).start()

    def gather_finish(mine, buf, send, recv):
        for d in range(groups):
            other = ((q + groups - d) % groups) * 2 + (1 - core)
            hop(mine, buf.at[other], send.at[d], recv.at[other], sibling).wait_recv()
        for d in range(1, 2 * groups):
            hop(mine, buf.at[c], send.at[d], recv.at[c], sibling).wait_send()

    def chain(i, source):
        return pltpu.make_async_remote_copy(
            src_ref=csend.at[i],
            dst_ref=crecv.at[source],
            send_sem=cs.at[i],
            recv_sem=cr.at[source],
            device_id={"rows": i},
            device_id_type=pl.DeviceIdType.MESH,
        )

    def stage(s):
        @pl.when(me == s)
        def _():
            x = x_ref[...]
            for j in range(peers_r - 1, s, -1):
                chain(s, j).wait_recv()
                x = x - crecv[j]
            w = jnp.dot(x, dinv_ref[...], precision=HIGH, preferred_element_type=F32)
            wown[...] = w.astype(BF16)
            for i in range(s - 1, -1, -1):
                csend[i] = jnp.dot(
                    w, fac_ref[:, i * width : (i + 1) * width], precision=HIGH, preferred_element_type=F32
                )
                chain(i, s).start()

    def cos_block(k, j, slot):
        rows = pl.ds(pl.multiple_of(j * FB, FB), FB)
        turns = jnp.dot(
            ft_ref[rows, :],
            g_ref[:, pl.ds(pl.multiple_of(k * CHUNK, CHUNK), CHUNK)],
            preferred_element_type=F32,
        )
        v = 0.25 - jnp.abs(turns - jnp.round(turns))
        u = v * v
        p = poly[3]
        for a in (poly[2], poly[1], poly[0]):
            p = p * u + a
        feat[slot, rows, :] = (p * v).astype(BF16)

    def exp_block(k, j, slot):
        turns = jnp.dot(
            ot_ref[pl.ds(pl.multiple_of(j * FB, FB), FB), :],
            g_ref[:, pl.ds(pl.multiple_of(k * CHUNK, CHUNK), CHUNK)],
            preferred_element_type=F32,
        )
        feat[slot, pl.ds(pl.multiple_of((j + nf) * FB, FB), FB), :] = jnp.exp2(turns).astype(BF16)

    def product(j, slot):
        cols = pl.ds(pl.multiple_of(j * FB, FB), FB)
        acc[...] += jnp.dot(coefw[:, cols], feat[slot, cols, :], preferred_element_type=F32)

    def features(k):
        pl.loop(0, nf)(lambda j: cos_block(k, j, k % slots))
        pl.loop(0, no)(lambda j: exp_block(k, j, k % slots))

    def share(k, to, source):
        return pltpu.make_async_remote_copy(
            src_ref=sbuf.at[k, to],
            dst_ref=rbuf.at[k, source],
            send_sem=ss.at[k, to],
            recv_sem=sr.at[k, source],
            device_id={"rows": to},
            device_id_type=pl.DeviceIdType.MESH,
        )

    def deliver(k):
        own[k] = acc[pl.ds(pl.multiple_of(me * part, part), part), :]
        for d in range(1, peers_r):
            to = (me + d) % peers_r
            sbuf[k, to] = acc[pl.ds(pl.multiple_of(to * part, part), part), :].astype(BF16)
            share(k, to, me).start()

    gather_send(coef_ref, cbuf, gs, gr)
    for s in range(peers_r - 1, -1, -1):
        stage(s)
        if s == 0:
            gather_send(wown, wbuf, ws, wr)
            gather_forward(coef_ref, cbuf, gs, gr)
        if peers_r - 1 - s < slots:
            features(peers_r - 1 - s)
    gather_forward(wown, wbuf, ws, wr)
    gather_finish(coef_ref, cbuf, gs, gr)
    for b in range(peers_c):
        wide[b * samples : (b + 1) * samples, : nf * FB] = cbuf[b].astype(F32)
    gather_finish(wown, wbuf, ws, wr)
    for b in range(peers_c):
        wide[b * samples : (b + 1) * samples, nf * FB :] = wbuf[b].astype(F32)
    coefw[...] = wide[...].astype(BF16)

    @pl.loop(0, chunks - slots)
    def _(k):
        slot = k % slots
        acc[...] = jnp.zeros_like(acc)

        @pl.loop(0, nf)
        def _(j):
            product(j, slot)
            cos_block(k + slots, j, slot)

        @pl.loop(0, no)
        def _(j):
            product(j + nf, slot)
            exp_block(k + slots, j, slot)

        deliver(k)

    @pl.loop(chunks - slots, chunks)
    def _(k):
        acc[...] = jnp.dot(coefw[...], feat[k % slots], preferred_element_type=F32)
        deliver(k)

    @pl.loop(0, chunks)
    def _(k):
        total = own[k]
        for d in range(1, peers_r):
            source = (me + d) % peers_r
            share(k, source, source).wait_recv()
            total = total + rbuf[k, source].astype(F32)
        out_ref[:, pl.ds(pl.multiple_of(k * CHUNK, CHUNK), CHUNK)] = total
        for d in range(1, peers_r):
            to = (me + d) % peers_r
            share(k, to, me).wait_send()

    for i in range(peers_r - 1):

        @pl.when(me > i)
        def _():
            chain(i, me).wait_send()


def rounded(a):
    return lax.reduce_precision(a, exponent_bits=8, mantissa_bits=7)


def pieces(a):
    first = rounded(a)
    second = rounded(a - first)
    return [first, second, rounded(a - first - second)]


def padded(rows):
    stacked = jnp.concatenate(rows, axis=0)
    return jnp.pad(stacked, ((0, DEPTH - stacked.shape[0]), (0, 0))).astype(BF16)


def body(whitened, factor_rows, diag_inv, observed, inv_length, grid_coords, frequencies, phases, prior_coef):
    peers_r = lax.axis_size("rows")
    peers_c = lax.axis_size("cand")
    feats = frequencies.shape[1]
    obs = observed.shape[1]
    cands = grid_coords.shape[1]
    samples, width = whitened.shape
    all_samples = samples * peers_c
    part = all_samples // peers_r
    chunks = cands // CHUNK
    slots = 4
    top = GRID - 1
    turn = 1.0 / (2 * np.pi)
    log2e = 1.0 / np.log(2.0)

    levels = grid_coords.astype(F32)
    l2 = (inv_length * inv_length)[:, None]
    per_cand = jnp.sum(levels * levels * l2, axis=0, keepdims=True) * (-0.5 * log2e / (top * top))
    per_obs = jnp.sum(observed * observed * l2, axis=0, keepdims=True) * (-0.5 * log2e)
    ones = jnp.ones((3, cands), F32)
    g = padded([levels, levels, levels, ones] + pieces(per_cand))
    ft = padded(pieces(frequencies * (turn / top)) + pieces(phases[None, :] * turn)).T
    ot = padded(
        pieces(observed * l2 * (log2e / top)) + pieces(per_obs) + [jnp.ones((3, obs), F32)]
    ).T
    scale = float(np.sqrt(2.0 / (feats * peers_r)))

    vmem = pl.BlockSpec(memory_space=pltpu.VMEM)
    dma = pltpu.SemaphoreType.DMA
    out = pl.pallas_call(
        functools.partial(kernel, peers_r, peers_c, scale),
        out_shape=jax.ShapeDtypeStruct((part, cands), F32),
        in_specs=[vmem] * 7,
        out_specs=vmem,
        scratch_shapes=[
            pltpu.VMEM((slots, feats + obs, CHUNK), BF16),
            pltpu.VMEM((all_samples, feats + obs), BF16),
            pltpu.VMEM((peers_c, samples, feats), BF16),
            pltpu.VMEM((samples, width), BF16),
            pltpu.VMEM((peers_c, samples, width), BF16),
            pltpu.VMEM((all_samples, feats + obs), F32),
            pltpu.VMEM((peers_r, samples, width), F32),
            pltpu.VMEM((peers_r, samples, width), F32),
            pltpu.VMEM((all_samples, CHUNK), F32),
            pltpu.VMEM((chunks, part, CHUNK), F32),
            pltpu.VMEM((chunks, peers_r, part, CHUNK), BF16),
            pltpu.VMEM((chunks, peers_r, part, CHUNK), BF16),
            dma((peers_c,)),
            dma((peers_c,)),
            dma((peers_c,)),
            dma((peers_c,)),
            dma((peers_r,)),
            dma((peers_r,)),
            dma((chunks, peers_r)),
            dma((chunks, peers_r)),
        ],
        compiler_params=pltpu.CompilerParams(
            collective_id=0, has_side_effects=True, vmem_limit_bytes=56 * 1024 * 1024
        ),
    )(g, ft, ot, prior_coef, whitened, factor_rows, diag_inv)
    return out.T


def solution(mesh):
    in_specs = (
        P("cand", "rows"),
        P("rows", None),
        P("rows", None),
        P(None, "rows"),
        P(),
        P(None, "cand"),
        P(None, "rows"),
        P("rows"),
        P("cand", "rows"),
    )
    out_specs = P("cand", "rows")
    return jax.shard_map(body, mesh=mesh, in_specs=in_specs, out_specs=out_specs, check_vma=False)
```

```python
import functools

import jax
import jax.numpy as jnp
import numpy as np
from jax import lax
from jax.experimental import pallas as pl
from jax.experimental.pallas import tpu as pltpu
from jax.sharding import PartitionSpec as P

GRID = 21
CHUNK = 512
FB = 256
FW = 1024
EW = 512
DEPTH = 128
SEG = 32
HIGH = lax.Precision.HIGHEST
F32 = jnp.float32
BF16 = jnp.bfloat16


def sine_coefficients(terms):
    v = 0.125 * (1 - np.cos(np.pi * (np.arange(400) + 0.5) / 400)) + 1e-9
    rows = np.stack([v ** (2 * i + 1) for i in range(terms)], 1)
    goal = np.sin(2 * np.pi * v)
    return np.linalg.lstsq(rows / goal[:, None], np.ones_like(goal), rcond=None)[0]


def pieces(a):
    first = a.astype(BF16).astype(F32)
    second = (a - first).astype(BF16).astype(F32)
    return [first, second, (a - first - second).astype(BF16).astype(F32)]


def kernel(
    peers_r,
    peers_c,
    scale,
    levels_ref,
    obs_ref,
    scale_ref,
    freq_ref,
    phase_ref,
    coef_ref,
    x_ref,
    fac_ref,
    dinv_ref,
    out_ref,
    g_ref,
    ft_ref,
    ot_ref,
    ctmp,
    ttmp,
    feat,
    coefw,
    cbuf,
    wown,
    wbuf,
    csend,
    crecv,
    acc,
    own,
    sbuf,
    rbuf,
    gs,
    gr,
    ws,
    wr,
    cs,
    cr,
    ss,
    sr,
):
    me = lax.axis_index("rows")
    c = lax.axis_index("cand")
    groups = peers_c // 2
    q = c // 2
    core = c % 2
    sibling = q * 2 + (1 - core)
    samples = coef_ref.shape[0]
    feats = ft_ref.shape[0]
    obs = ot_ref.shape[0]
    slots = feat.shape[0]
    chunks = out_ref.shape[1] // CHUNK
    part = out_ref.shape[0]
    width = x_ref.shape[1]
    poly = [float(a) * scale for a in sine_coefficients(4)]

    barrier = pltpu.get_barrier_semaphore()
    for d in range(1, peers_r):
        pl.semaphore_signal(
            barrier, inc=1, device_id={"rows": (me + d) % peers_r}, device_id_type=pl.DeviceIdType.MESH
        )
    for d in range(1, groups):
        pl.semaphore_signal(
            barrier,
            inc=1,
            device_id={"cand": ((q + d) % groups) * 2 + core},
            device_id_type=pl.DeviceIdType.MESH,
        )
    pl.semaphore_signal(barrier, inc=1, device_id={"cand": sibling}, device_id_type=pl.DeviceIdType.MESH)
    pl.semaphore_wait(barrier, peers_r - 1 + groups)

    def hop(src, dst, send, recv, cand):
        return pltpu.make_async_remote_copy(
            src_ref=src,
            dst_ref=dst,
            send_sem=send,
            recv_sem=recv,
            device_id={"cand": cand},
            device_id_type=pl.DeviceIdType.MESH,
        )

    def gather_send(mine, buf, send, recv):
        for d in range(1, groups):
            hop(mine, buf.at[c], send.at[d], recv.at[c], ((q + d) % groups) * 2 + core).start()
        hop(mine, buf.at[c], send.at[groups], recv.at[c], sibling).start()
        buf[c] = mine[...]

    def gather_forward(mine, buf, send, recv):
        for d in range(1, groups):
            other = ((q + groups - d) % groups) * 2 + core
            hop(mine, buf.at[other], send.at[d], recv.at[other], sibling).wait_recv()
            hop(buf.at[other], buf.at[other], send.at[groups + d], recv.at[other], sibling).start()

    def gather_finish(mine, buf, send, recv):
        for d in range(groups):
            other = ((q + groups - d) % groups) * 2 + (1 - core)
            hop(mine, buf.at[other], send.at[d], recv.at[other], sibling).wait_recv()
        for d in range(1, 2 * groups):
            hop(mine, buf.at[c], send.at[d], recv.at[c], sibling).wait_send()

    def chain(i, source):
        return pltpu.make_async_remote_copy(
            src_ref=csend.at[i],
            dst_ref=crecv.at[source],
            send_sem=cs.at[i],
            recv_sem=cr.at[source],
            device_id={"rows": i},
            device_id_type=pl.DeviceIdType.MESH,
        )

    def stage(s):
        @pl.when(me == s)
        def _():
            x = x_ref[...]
            for j in range(peers_r - 1, s, -1):
                chain(s, j).wait_recv()
                x = x - crecv[j]
            w = jnp.dot(x, dinv_ref[...], precision=HIGH, preferred_element_type=F32)
            wown[...] = w.astype(BF16)
            for i in range(s - 1, -1, -1):
                csend[i] = jnp.dot(
                    w, fac_ref[:, i * width : (i + 1) * width], precision=HIGH, preferred_element_type=F32
                )
                chain(i, s).start()

    def angles(k, source, start, size):
        return jnp.dot(
            source[pl.ds(start, size), :],
            g_ref[:, pl.ds(pl.multiple_of(k * CHUNK, CHUNK), CHUNK)],
            preferred_element_type=F32,
        )

    def cos_block(k, j, slot):
        start = pl.multiple_of(j * FW, FW)
        turns = angles(k, ft_ref, start, FW)
        v = 0.25 - jnp.abs(turns - jnp.round(turns))
        u = v * v
        p = poly[3]
        for a in (poly[2], poly[1], poly[0]):
            p = p * u + a
        feat[slot, pl.ds(start, FW), :] = (p * v).astype(BF16)

    def exp_block(k, j, slot):
        start = pl.multiple_of(j * EW, EW)
        turns = angles(k, ot_ref, start, EW)
        feat[slot, pl.ds(pl.multiple_of(feats + start, EW), EW), :] = jnp.exp2(turns).astype(BF16)

    def product(start, size, slot):
        cols = pl.ds(pl.multiple_of(start, size), size)
        acc[...] += jnp.dot(coefw[:, cols], feat[slot, cols, :], preferred_element_type=F32)

    def features(k):
        pl.loop(0, feats // FW)(lambda j: cos_block(k, j, k % slots))
        pl.loop(0, obs // EW)(lambda j: exp_block(k, j, k % slots))

    def share(k, to, source):
        return pltpu.make_async_remote_copy(
            src_ref=sbuf.at[k, to],
            dst_ref=rbuf.at[k, source],
            send_sem=ss.at[k, to],
            recv_sem=sr.at[k, source],
            device_id={"rows": to},
            device_id_type=pl.DeviceIdType.MESH,
        )

    def deliver(k):
        own[k] = acc[pl.ds(pl.multiple_of(me * part, part), part), :]
        for d in range(1, peers_r):
            to = (me + d) % peers_r
            sbuf[k, to] = acc[pl.ds(pl.multiple_of(to * part, part), part), :].astype(BF16)
            share(k, to, me).start()

    gather_send(coef_ref, cbuf, gs, gr)

    dim = levels_ref.shape[0]
    top = GRID - 1
    turn = 1.0 / (2 * np.pi)
    log2e = 1.0 / np.log(2.0)
    l2 = scale_ref[...] * scale_ref[...]
    ctmp[...] = jnp.zeros_like(ctmp)
    ttmp[...] = jnp.zeros_like(ttmp)

    @pl.loop(0, feats // FB)
    def _(j):
        cols = pl.ds(pl.multiple_of(j * FB, FB), FB)
        for i, piece in enumerate(pieces(freq_ref[:, cols] * (turn / top))):
            ttmp[SEG * i : SEG * i + dim, :] = piece
        for i, piece in enumerate(pieces(phase_ref[:, cols] * turn)):
            ttmp[3 * SEG + i : 3 * SEG + i + 1, :] = piece
        ft_ref[cols, :] = jnp.transpose(ttmp[...]).astype(BF16)

    ttmp[3 * SEG + 3 : 3 * SEG + 6, :] = jnp.ones((3, FB), F32)

    @pl.loop(0, obs // FB)
    def _(j):
        cols = pl.ds(pl.multiple_of(j * FB, FB), FB)
        seen = obs_ref[:, cols]
        for i, piece in enumerate(pieces(seen * l2 * (log2e / top))):
            ttmp[SEG * i : SEG * i + dim, :] = piece
        norm = jnp.sum(seen * seen * l2, axis=0, keepdims=True) * (-0.5 * log2e)
        for i, piece in enumerate(pieces(norm)):
            ttmp[3 * SEG + i : 3 * SEG + i + 1, :] = piece
        ot_ref[cols, :] = jnp.transpose(ttmp[...]).astype(BF16)

    @pl.loop(0, chunks)
    def _(k):
        cols = pl.ds(pl.multiple_of(k * CHUNK, CHUNK), CHUNK)
        levels = levels_ref[:, cols].astype(F32)
        ctmp[0:dim, :] = levels
        low = ctmp[...].astype(BF16)
        norm = jnp.sum(levels * levels * l2, axis=0, keepdims=True) * (-0.5 * log2e / (top * top))
        row = lax.broadcasted_iota(jnp.int32, (SEG, CHUNK), 0)
        tail = jnp.where(row < 3, 1.0, 0.0)
        for i, piece in enumerate(pieces(norm)):
            tail = jnp.where(row == 3 + i, piece, tail)
        for i in range(3):
            g_ref[SEG * i : SEG * (i + 1), cols] = low
        g_ref[3 * SEG :, cols] = tail.astype(BF16)

    for s in range(peers_r - 1, -1, -1):
        stage(s)
        if s == 0:
            gather_send(wown, wbuf, ws, wr)
            gather_forward(coef_ref, cbuf, gs, gr)
        if peers_r - 1 - s < slots:
            features(peers_r - 1 - s)
    gather_forward(wown, wbuf, ws, wr)
    gather_finish(coef_ref, cbuf, gs, gr)
    gather_finish(wown, wbuf, ws, wr)
    for buf, cols in ((cbuf, slice(0, feats)), (wbuf, slice(feats, feats + obs))):
        for b in range(0, peers_c, max(1, 16 // samples)):
            if samples % 16 == 0:
                coefw[b * samples : (b + 1) * samples, cols] = buf[b]
            else:
                group = [buf[b + i].astype(F32) for i in range(16 // samples)]
                coefw[b * samples : b * samples + 16, cols] = jnp.concatenate(group, axis=0).astype(BF16)

    @pl.loop(0, chunks - slots)
    def _(k):
        slot = k % slots
        acc[...] = jnp.zeros_like(acc)

        @pl.loop(0, feats // FW)
        def _(j):
            product(j * FW, FW, slot)
            cos_block(k + slots, j, slot)

        @pl.loop(0, obs // EW)
        def _(j):
            product(feats + j * EW, EW, slot)
            exp_block(k + slots, j, slot)

        deliver(k)

    @pl.loop(chunks - slots, chunks)
    def _(k):
        acc[...] = jnp.dot(coefw[...], feat[k % slots], preferred_element_type=F32)
        deliver(k)

    @pl.loop(0, chunks)
    def _(k):
        total = own[k]
        for d in range(1, peers_r):
            source = (me + d) % peers_r
            share(k, source, source).wait_recv()
            total = total + rbuf[k, source].astype(F32)
        out_ref[:, pl.ds(pl.multiple_of(k * CHUNK, CHUNK), CHUNK)] = total
        for d in range(1, peers_r):
            to = (me + d) % peers_r
            share(k, to, me).wait_send()

    for i in range(peers_r - 1):

        @pl.when(me > i)
        def _():
            chain(i, me).wait_send()


def body(whitened, factor_rows, diag_inv, observed, inv_length, grid_coords, frequencies, phases, prior_coef):
    peers_r = lax.axis_size("rows")
    peers_c = lax.axis_size("cand")
    feats = frequencies.shape[1]
    obs = observed.shape[1]
    cands = grid_coords.shape[1]
    samples, width = whitened.shape
    all_samples = samples * peers_c
    part = all_samples // peers_r
    chunks = cands // CHUNK
    slots = 4
    scale = float(np.sqrt(2.0 / (feats * peers_r)))

    vmem = pl.BlockSpec(memory_space=pltpu.VMEM)
    dma = pltpu.SemaphoreType.DMA
    out = pl.pallas_call(
        functools.partial(kernel, peers_r, peers_c, scale),
        out_shape=jax.ShapeDtypeStruct((part, cands), F32),
        in_specs=[vmem] * 9,
        out_specs=vmem,
        scratch_shapes=[
            pltpu.VMEM((DEPTH, cands), BF16),
            pltpu.VMEM((feats, DEPTH), BF16),
            pltpu.VMEM((obs, DEPTH), BF16),
            pltpu.VMEM((SEG, CHUNK), F32),
            pltpu.VMEM((DEPTH, FB), F32),
            pltpu.VMEM((slots, feats + obs, CHUNK), BF16),
            pltpu.VMEM((all_samples, feats + obs), BF16),
            pltpu.VMEM((peers_c, samples, feats), BF16),
            pltpu.VMEM((samples, width), BF16),
            pltpu.VMEM((peers_c, samples, width), BF16),
            pltpu.VMEM((peers_r, samples, width), F32),
            pltpu.VMEM((peers_r, samples, width), F32),
            pltpu.VMEM((all_samples, CHUNK), F32),
            pltpu.VMEM((chunks, part, CHUNK), F32),
            pltpu.VMEM((chunks, peers_r, part, CHUNK), BF16),
            pltpu.VMEM((chunks, peers_r, part, CHUNK), BF16),
            dma((peers_c,)),
            dma((peers_c,)),
            dma((peers_c,)),
            dma((peers_c,)),
            dma((peers_r,)),
            dma((peers_r,)),
            dma((chunks, peers_r)),
            dma((chunks, peers_r)),
        ],
        compiler_params=pltpu.CompilerParams(
            collective_id=0, has_side_effects=True, vmem_limit_bytes=56 * 1024 * 1024
        ),
    )(
        grid_coords,
        observed,
        inv_length[:, None],
        frequencies,
        phases[None, :],
        prior_coef,
        whitened,
        factor_rows,
        diag_inv,
    )
    return out.T


def solution(mesh):
    in_specs = (
        P("cand", "rows"),
        P("rows", None),
        P("rows", None),
        P(None, "rows"),
        P(),
        P(None, "cand"),
        P(None, "rows"),
        P("rows"),
        P("cand", "rows"),
    )
    out_specs = P("cand", "rows")
    return jax.shard_map(body, mesh=mesh, in_specs=in_specs, out_specs=out_specs, check_vma=False)
```
